32 devices in a mesh: leaf: 8 (over z, x), row: 4 (over y, core).
Axes of the slice: x: 2, y: 2, z: 4, core: 2. Of those that a mesh axis runs over, the one named last changes fastest.
Arguments:
- leaf_probes: bfloat16 [8, 2048, 128], P('leaf', 'row'), may hold values from -6 to 6
- lower_probes: bfloat16 [4, 4096, 128], P(None, ('leaf', 'row')), may hold values from -6 to 6
- middle_probes: bfloat16 [2, 8192, 128], P(None, ('leaf', 'row')), may hold values from -6 to 6
- root_probes: bfloat16 [16384, 128], P(('leaf', 'row')), may hold values from -6 to 6
- leaf_inverse: bfloat16 [8, 2048, 2048], P('leaf', 'row'), as said below
- lower_inverse: bfloat16 [4, 4096, 4096], P(None, 'row', 'leaf'), as said below
- middle_inverse: bfloat16 [2, 8192, 8192], P(None, 'row', 'leaf'), as said below
- root_inverse: bfloat16 [16384, 16384], P('row', 'leaf'), as said below
- leaf_panel: bfloat16 [8, 512, 2048], P('leaf', 'row'), may hold values from -0.09375 to 0.09375
- lower_to_middle: bfloat16 [4, 8192, 4096], P(None, 'leaf', 'row'), may hold values from -0.09375 to 0.09375
- lower_to_root: bfloat16 [4, 16384, 4096], P(None, 'leaf', 'row'), may hold values from -0.09375 to 0.09375
- middle_to_root: bfloat16 [2, 16384, 8192], P(None, 'leaf', 'row'), may hold values from -0.0625 to 0.0625
- leaf_parent: int32 [8], replicated, may hold values from 0 to 3
- leaf_blocks: int32 [8, 4], replicated, may hold values from 0 to 127, as said below
Outputs:
- leaf_solution: bfloat16 [8, 2048, 128], P('leaf', 'row')
- lower_solution: bfloat16 [4, 4096, 128], P(None, ('leaf', 'row'))
- middle_solution: bfloat16 [2, 8192, 128], P(None, ('leaf', 'row'))
- root_solution: bfloat16 [16384, 128], P(('leaf', 'row'))
The draws below stay inside these ranges and needn't reach their ends.
Inputs may be any that keep to these rules, and one draw needn't show every extreme that they name: `leaf_inverse`: every inverse of a diagonal factor block is lower triangular: entries above its diagonal are zero. `lower_inverse`: every inverse of a diagonal factor block is lower triangular: entries above its diagonal are zero. `middle_inverse`: every inverse of a diagonal factor block is lower triangular: entries above its diagonal are zero. `root_inverse`: every inverse of a diagonal factor block is lower triangular: entries above its diagonal are zero. `leaf_blocks`: columns 0 and 1 are two different blocks of 128 rows of the parent separator, column 2 a block of the second-level separator above it, column 3 a block of the root.
All inputs are finite; a program needn't handle non-finite values.
Results may differ from the reference program's by a relative error of at most 0.04.
Values may be sent and summed in bfloat16 or wider, within the bound.
A program may use at most 128 MiB of HBM per device.

```python
import math
import jax
import jax.numpy as jnp
import numpy as np
from jax import lax

PROBES = 128
LEAF_ORDER = 2048
LOWER_ORDER = 4096
MIDDLE_ORDER = 8192
ROOT_ORDER = 16384
BLOCK = 128
PANEL = 512
LEAVES = 8


def triangle_draw(key, members, matrix_order):
    key_below, key_middle = jax.random.split(key)
    full_shape = (members, matrix_order, matrix_order)
    values = jax.random.normal(key_below, full_shape, jnp.float32)
    leading = jax.random.uniform(key_middle, (members, matrix_order, 1), jnp.float32, 0.6, 1.4)
    row_ids = lax.broadcasted_iota(jnp.int32, (1, matrix_order, 1), 1)
    column_ids = lax.broadcasted_iota(jnp.int32, (1, 1, matrix_order), 2)
    below = jnp.where(column_ids < row_ids, values * (0.6 / math.sqrt(matrix_order)), 0.0)
    return below + jnp.where(column_ids == row_ids, leading, 0.0)


def draw_leaf_inverse(key, part):
    return triangle_draw(key, LEAVES, LEAF_ORDER).astype(jnp.bfloat16)


def draw_lower_inverse(key, part):
    return triangle_draw(key, 4, LOWER_ORDER).astype(jnp.bfloat16)


def draw_middle_inverse(key, part):
    return triangle_draw(key, 2, MIDDLE_ORDER).astype(jnp.bfloat16)


def draw_root_inverse(key, part):
    return triangle_draw(key, 1, ROOT_ORDER)[0].astype(jnp.bfloat16)


def draw_leaf_blocks(key, part):
    key_list = jax.random.split(key, 4)
    lower_count = LOWER_ORDER // BLOCK
    first_block = jax.random.randint(key_list[0], (LEAVES, 1), 0, lower_count)
    second_block = (first_block + jax.random.randint(key_list[1], (LEAVES, 1), 1, lower_count)) % lower_count
    middle_block = jax.random.randint(key_list[2], (LEAVES, 1), 0, MIDDLE_ORDER // BLOCK)
    middle_block = middle_block.at[0, 0].set(0)
    root_block = jax.random.randint(key_list[3], (LEAVES, 1), 0, ROOT_ORDER // BLOCK)
    root_block = root_block.at[0, 0].set(ROOT_ORDER // BLOCK - 1)
    return jnp.concatenate([first_block, second_block, middle_block, root_block], axis=1).astype(jnp.int32)


def place_ends(entries, own_key, low, top_value):
    longest = entries.shape.index(max(entries.shape))
    spots = []
    for shift in (0, 1):
        where = [jax.random.randint(jax.random.fold_in(own_key, axis), (), 0, length) for axis, length in enumerate(entries.shape)]
        where[longest] = (where[longest] + shift) % entries.shape[longest]
        spots.append(tuple(where))
    return entries.at[spots[0]].set(low).at[spots[1]].set(top_value)


def with_spikes(drawn, stream_key, source, target, parts, factor):
    def block_of(position):
        return (jnp.arange(drawn.shape[position]) // (drawn.shape[position] // parts)).reshape((-1,) + (1,) * (drawn.ndim - 1 - position))

    first = jax.random.permutation(stream_key, parts)[block_of(target)]
    other_side = (block_of(target) + parts // 2) % parts
    return jnp.where((block_of(source) == first) | (block_of(source) == other_side), factor * drawn, drawn)


def block_scale(stream_key, dims, cuts, least, high):
    gain, own = 1.0, jax.random.fold_in(stream_key, 6)
    for axis_at, blocks in cuts:
        draws = jnp.exp(jax.random.uniform(jax.random.fold_in(own, axis_at), (blocks,), jnp.float32, least / len(cuts), high / len(cuts)))
        gain = gain * jnp.repeat(draws, dims[axis_at] // blocks).reshape([-1 if axis == axis_at else 1 for axis in range(len(dims))])
    return gain


def rank_table(amount, slope):
    loads = [(1 << 20) // math.isqrt(grade ** slope) + 1 for grade in range(1, amount + 1)]
    width = 1 + sum(loads) // (1 << 30)
    return np.cumsum(np.array([max(1, weight // width) for weight in loads]))


def skewed_ids(rng, dims, amount, skew):
    table = rank_table(amount, skew)
    lot = jax.random.randint(jax.random.fold_in(rng, 1), dims, 0, int(table[amount - 1]))
    grade = jnp.searchsorted(jnp.asarray(table, jnp.int32), lot, side="right")
    return jax.random.permutation(jax.random.fold_in(rng, 2), amount)[grade].astype(jnp.int32)


def scatter_about(rng, extent, width, reach, shards=(), held_as=jnp.bfloat16):
    entries = width * jax.random.normal(rng, extent, jnp.float32)
    if shards:
        entries = entries * block_scale(rng, extent, shards, -0.22, 0.18)
    return jnp.clip(entries, -reach, reach).astype(held_as)


def heavy_noise(key, dims, scale, limit, pieces, heavy, kind=jnp.bfloat16):
    values = scale * jax.random.normal(key, dims, jnp.float32)
    if pieces:
        values = values * block_scale(key, dims, pieces, -0.22, 0.18)
    return jnp.clip(with_spikes(values, jax.random.fold_in(key, 3), *heavy), -limit, limit).astype(kind)


def setup_inputs(seed: int = 0) -> dict:
    seeds = jax.random.split(jax.random.key(seed), 15)
    leaf_probes = scatter_about(seeds[0], (LEAVES, LEAF_ORDER, PROBES), 1.0, 6.0, ((0, 8), (1, 4)))
    lower_probes = scatter_about(seeds[1], (4, LOWER_ORDER, PROBES), 1.0, 6.0, ((1, 32),))
    middle_probes = scatter_about(seeds[2], (2, MIDDLE_ORDER, PROBES), 1.0, 6.0, ((1, 32),))
    root_probes = scatter_about(seeds[3], (ROOT_ORDER, PROBES), 1.0, 6.0, ((0, 32),))
    leaf_inverse = draw_leaf_inverse(jax.random.fold_in(seeds[14], 71), 0)
    lower_inverse = draw_lower_inverse(jax.random.fold_in(seeds[14], 71), 0)
    middle_inverse = draw_middle_inverse(jax.random.fold_in(seeds[14], 71), 0)
    root_inverse = draw_root_inverse(jax.random.fold_in(seeds[14], 71), 0)
    leaf_panel = scatter_about(seeds[8], (LEAVES, PANEL, LEAF_ORDER), (2 * LEAF_ORDER) ** -0.5, 0.09375, ((0, 8), (1, 4)))
    lower_to_middle = heavy_noise(seeds[9], (4, MIDDLE_ORDER, LOWER_ORDER), (2 * LOWER_ORDER) ** -0.5, 0.09375, ((1, 8), (2, 4)), (1, 2, 8, 2.0))
    lower_to_root = heavy_noise(seeds[10], (4, ROOT_ORDER, LOWER_ORDER), (2 * LOWER_ORDER) ** -0.5, 0.09375, ((1, 8), (2, 4)), (1, 2, 8, 2.0))
    middle_to_root = heavy_noise(seeds[11], (2, ROOT_ORDER, MIDDLE_ORDER), (2 * MIDDLE_ORDER) ** -0.5, 0.0625, ((1, 8), (2, 4)), (1, 2, 8, 2.0))
    leaf_parent = place_ends(skewed_ids(seeds[12], (LEAVES,), 4, 2), jax.random.fold_in(seeds[12], 3), 0, 3).astype(jnp.int32)
    leaf_blocks = draw_leaf_blocks(jax.random.fold_in(seeds[14], 71), 0)
    return {"leaf_probes": leaf_probes, "lower_probes": lower_probes, "middle_probes": middle_probes, "root_probes": root_probes, "leaf_inverse": leaf_inverse, "lower_inverse": lower_inverse, "middle_inverse": middle_inverse, "root_inverse": root_inverse, "leaf_panel": leaf_panel, "lower_to_middle": lower_to_middle, "lower_to_root": lower_to_root, "middle_to_root": middle_to_root, "leaf_parent": leaf_parent, "leaf_blocks": leaf_blocks}


def product(left, right):
    return jnp.dot(left, right, preferred_element_type=jnp.float32)


def rounded(values):
    return lax.optimization_barrier(values.astype(jnp.bfloat16)).astype(jnp.float32)


def target_rows(leaf_parent, leaf_blocks):
    offsets = jnp.arange(BLOCK, dtype=jnp.int32)[None, :]
    parent_base = leaf_parent * LOWER_ORDER
    first_rows = (parent_base + leaf_blocks[:, 0] * BLOCK)[:, None] + offsets
    second_rows = (parent_base + leaf_blocks[:, 1] * BLOCK)[:, None] + offsets
    middle_rows = ((leaf_parent // 2) * MIDDLE_ORDER + leaf_blocks[:, 2] * BLOCK)[:, None] + offsets
    root_rows = (leaf_blocks[:, 3] * BLOCK)[:, None] + offsets
    return first_rows, second_rows, middle_rows, root_rows


def reference(leaf_probes, lower_probes, middle_probes, root_probes, leaf_inverse, lower_inverse, middle_inverse, root_inverse, leaf_panel, lower_to_middle, lower_to_root, middle_to_root, leaf_parent, leaf_blocks):
    probe_count = leaf_probes.shape[-1]
    leaf_solved = jnp.einsum("lab,lbp->lap", leaf_inverse.astype(jnp.float32), leaf_probes.astype(jnp.float32)).astype(jnp.bfloat16)
    leaf_update = rounded(jnp.einsum("lkb,lbp->lkp", leaf_panel.astype(jnp.float32), leaf_solved.astype(jnp.float32)))
    first_rows, second_rows, middle_rows, root_rows = target_rows(leaf_parent, leaf_blocks)

    def panel_block(number):
        return leaf_update[:, number * BLOCK:(number + 1) * BLOCK].reshape(-1, probe_count)

    lower_added = jnp.zeros((4 * LOWER_ORDER, probe_count), jnp.float32)
    lower_added = lower_added.at[first_rows.reshape(-1)].add(panel_block(0))
    lower_added = lower_added.at[second_rows.reshape(-1)].add(panel_block(1))
    middle_added = jnp.zeros((2 * MIDDLE_ORDER, probe_count), jnp.float32).at[middle_rows.reshape(-1)].add(panel_block(2))
    root_added = jnp.zeros((ROOT_ORDER, probe_count), jnp.float32).at[root_rows.reshape(-1)].add(panel_block(3))

    lower_input = (lower_probes.astype(jnp.float32) - lower_added.reshape(4, LOWER_ORDER, probe_count)).astype(jnp.bfloat16)
    lower_solved = jnp.stack([product(lower_inverse[member], lower_input[member]) for member in range(4)]).astype(jnp.bfloat16)
    lower_terms = [product(lower_to_middle[member], lower_solved[member]) for member in range(4)]
    middle_total = middle_added.reshape(2, MIDDLE_ORDER, probe_count) + jnp.stack([lower_terms[0] + lower_terms[1], lower_terms[2] + lower_terms[3]])
    middle_input = (middle_probes.astype(jnp.float32) - middle_total).astype(jnp.bfloat16)
    middle_solved = jnp.stack([product(middle_inverse[member], middle_input[member]) for member in range(2)]).astype(jnp.bfloat16)
    root_total = root_added
    for member in range(4):
        root_total = root_total + product(lower_to_root[member], lower_solved[member])
    for member in range(2):
        root_total = root_total + product(middle_to_root[member], middle_solved[member])
    root_input = (root_probes.astype(jnp.float32) - root_total).astype(jnp.bfloat16)
    root_solved = product(root_inverse, root_input).astype(jnp.bfloat16)

    root_solution = product(root_inverse.T, root_solved).astype(jnp.bfloat16)
    middle_reduced = jnp.stack([middle_solved[member].astype(jnp.float32) - product(middle_to_root[member].T, root_solution) for member in range(2)]).astype(jnp.bfloat16)
    middle_solution = jnp.stack([product(middle_inverse[member].T, middle_reduced[member]) for member in range(2)]).astype(jnp.bfloat16)
    lower_reduced = jnp.stack([lower_solved[member].astype(jnp.float32) - product(lower_to_middle[member].T, middle_solution[member // 2]) - product(lower_to_root[member].T, root_solution) for member in range(4)]).astype(jnp.bfloat16)
    lower_solution = jnp.stack([product(lower_inverse[member].T, lower_reduced[member]) for member in range(4)]).astype(jnp.bfloat16)

    lower_flat = lower_solution.reshape(-1, probe_count)
    middle_flat = middle_solution.reshape(-1, probe_count)
    ancestor = jnp.concatenate([lower_flat[first_rows], lower_flat[second_rows], middle_flat[middle_rows], root_solution[root_rows]], axis=1)
    leaf_back = jnp.einsum("lkb,lkp->lbp", leaf_panel.astype(jnp.float32), ancestor.astype(jnp.float32))
    leaf_reduced = (leaf_solved.astype(jnp.float32) - leaf_back).astype(jnp.bfloat16)
    leaf_solution = jnp.einsum("lab,lap->lbp", leaf_inverse.astype(jnp.float32), leaf_reduced.astype(jnp.float32)).astype(jnp.bfloat16)
    return leaf_solution, lower_solution, middle_solution, root_solution
```

```python
import functools

import jax
import jax.numpy as jnp
from jax import lax
from jax.experimental import pallas as pl
from jax.experimental.pallas import tpu as pltpu
from jax.sharding import PartitionSpec as P

LOWER_ORDER = 4096
MIDDLE_ORDER = 8192
ROOT_ORDER = 16384
BLOCK = 128
PANEL = 512
LEVELS = 4


def exchange_kernel(axis, n, reduce, gather, has_base, *refs):
    refs = list(refs)
    parts_ref = refs.pop(0)
    base_ref = refs.pop(0) if has_base else None
    out_ref = refs.pop(0)
    near_land, staged, far_land, whole, sems = refs
    far_count = n // 2
    me = lax.axis_index(axis)
    near = lax.rem(me, 2)
    far = me // 2
    partner = far * 2 + (1 - near)

    def far_at(k):
        return lax.rem(far + k, far_count)

    def device(index):
        return {axis: index}

    def remote(src, dst, kind, k, target):
        return pltpu.make_async_remote_copy(
            src_ref=src,
            dst_ref=dst,
            send_sem=sems.at[0, kind, k],
            recv_sem=sems.at[1, kind, k],
            device_id=device(target),
            device_id_type=pl.DeviceIdType.MESH,
        )

    barrier = pltpu.get_barrier_semaphore()
    pl.semaphore_signal(
        barrier, inc=1, device_id=device(partner), device_id_type=pl.DeviceIdType.MESH
    )
    for k in range(1, far_count):
        pl.semaphore_signal(
            barrier,
            inc=1,
            device_id=device(far_at(k) * 2 + near),
            device_id_type=pl.DeviceIdType.MESH,
        )
    pl.semaphore_wait(barrier, far_count)

    order = list(range(1, far_count)) + [0]
    sends = []
    if reduce:
        to_partner = {}
        for k in order:
            to_partner[k] = remote(
                parts_ref.at[:, far_at(k) * 2 + (1 - near)], near_land.at[k], 0, k, partner
            )
            to_partner[k].start()
        to_far = {}
        total = None
        for k in order:
            to_partner[k].wait_recv()
            pair = parts_ref[:, far_at(k) * 2 + near].astype(jnp.float32) + near_land[k].astype(
                jnp.float32
            )
            if k == 0:
                total = pair
            else:
                staged[k] = pair.astype(staged.dtype)
                to_far[k] = remote(
                    staged.at[k], far_land.at[k], 1, k, far_at(k) * 2 + near
                )
                to_far[k].start()
        for k in range(1, far_count):
            to_far[k].wait_recv()
            total = total + far_land[k].astype(jnp.float32)
        if has_base:
            total = base_ref[...] - total
        mine = total.astype(out_ref.dtype)
        sends += [to_partner[k] for k in order] + [to_far[k] for k in range(1, far_count)]
    else:
        mine = parts_ref[...]
    if gather:
        whole[:, me] = mine
        along = {}
        for k in range(1, far_count):
            along[k] = remote(whole.at[:, me], whole.at[:, me], 2, k, far_at(k) * 2 + near)
            along[k].start()
        passed = {0: remote(whole.at[:, me], whole.at[:, me], 3, 0, partner)}
        passed[0].start()
        for k in range(1, far_count):
            along[k].wait_recv()
            came = lax.rem(far + far_count - k, far_count) * 2 + near
            passed[k] = remote(whole.at[:, came], whole.at[:, came], 3, k, partner)
            passed[k].start()
        for k in range(far_count):
            passed[k].wait_recv()
        sends += [along[k] for k in range(1, far_count)] + [passed[k] for k in range(far_count)]
    for copy in sends:
        copy.wait_send()
    out_ref[...] = whole[...] if gather else mine


class Exchanges:
    def __init__(self):
        self.calls = 0

    def run(self, parts, axis, reduce, gather, base=None):
        n = lax.axis_size(axis)
        if reduce:
            s, rows, p = parts.shape
            w = rows // n
            operands = [parts.astype(jnp.bfloat16).reshape(s, n, w, p)]
        else:
            s, w, p = parts.shape
            operands = [parts]
        if base is not None:
            operands.append(base)
        far_count = n // 2
        slots = (far_count if reduce else 1, s if reduce else 1, w if reduce else 16, p)
        out_shape = (s, n, w, p) if gather else (s, w, p)
        whole_shape = (s, n, w, p) if gather else (1, 1, 16, p)
        call_id = self.calls
        self.calls += 1
        out = pl.pallas_call(
            functools.partial(exchange_kernel, axis, n, reduce, gather, base is not None),
            out_shape=jax.ShapeDtypeStruct(out_shape, jnp.bfloat16),
            in_specs=[pl.BlockSpec(memory_space=pltpu.VMEM)] * len(operands),
            out_specs=pl.BlockSpec(memory_space=pltpu.VMEM),
            scratch_shapes=[
                pltpu.VMEM(slots, jnp.bfloat16),
                pltpu.VMEM(slots, jnp.bfloat16),
                pltpu.VMEM(slots, jnp.bfloat16),
                pltpu.VMEM(whole_shape, jnp.bfloat16),
                pltpu.SemaphoreType.DMA((2, 4, far_count)),
            ],
            compiler_params=pltpu.CompilerParams(
                collective_id=call_id, has_side_effects=True, vmem_limit_bytes=16 << 20
            ),
            name=f"exchange_{axis}_{call_id}",
        )(*operands)
        return out.reshape(s, n * w, p) if gather else out

    def gather(self, pieces, axis):
        return self.run(pieces, axis, False, True)

    def total(self, summands, axis, base=None):
        return self.run(summands, axis, True, False, base)

    def everywhere(self, summands, axis, base=None):
        return self.run(summands, axis, True, True, base)


def product(spec, left, right):
    return jnp.einsum(spec, left, right, preferred_element_type=jnp.float32)


def target_places(leaf_parent, leaf_blocks, block_index):
    offset = jnp.arange(BLOCK, dtype=jnp.int32)[None, :]
    owners = leaf_parent if block_index < 2 else leaf_parent // 2
    if block_index == 3:
        owners = jnp.zeros_like(leaf_parent)
    owners = owners[:, None] + 0 * offset
    return owners, leaf_blocks[:, block_index : block_index + 1] * BLOCK + offset


def picker(leaf_parent, leaf_blocks, block_indices, row_devices, separators, start, window):
    slots = []
    for block_index in block_indices:
        owners, places = target_places(leaf_parent, leaf_blocks, block_index)
        inside = (places >= start) & (places < start + window)
        slot = jnp.where(inside, owners * window + places - start, -1)
        leaves = slot.shape[0]
        pieces = row_devices // LEVELS
        slots.append(slot.reshape(leaves, pieces, BLOCK // pieces).transpose(1, 0, 2).reshape(-1))
    slot = jnp.concatenate(slots)
    slot_ids = jnp.arange(separators * window, dtype=jnp.int32)
    return (slot_ids[:, None] == slot[None, :]).astype(jnp.bfloat16)


def body(
    leaf_probes,
    lower_probes,
    middle_probes,
    root_probes,
    leaf_inverse,
    lower_inverse,
    middle_inverse,
    root_inverse,
    leaf_panel,
    lower_to_middle,
    lower_to_root,
    middle_to_root,
    leaf_parent,
    leaf_blocks,
):
    f32, bf16 = jnp.float32, jnp.bfloat16
    links = Exchanges()
    leaf_devices = lax.axis_size("leaf")
    row_devices = lax.axis_size("row")
    position = lax.axis_index("leaf") * row_devices + lax.axis_index("row")
    devices = leaf_devices * row_devices
    probe_count = leaf_probes.shape[-1]
    counts = (4, 2, 1)
    windows = [order // devices for order in (LOWER_ORDER, MIDDLE_ORDER, ROOT_ORDER)]
    blocks_of = ((0, 1), (2,), (3,))
    pickers = [
        picker(
            leaf_parent,
            leaf_blocks,
            blocks_of[m],
            row_devices,
            counts[m],
            position * windows[m],
            windows[m],
        )
        for m in range(3)
    ]
    per_block = leaf_devices * BLOCK
    spans = ((0, 2 * per_block), (2 * per_block, 3 * per_block), (3 * per_block, 4 * per_block))

    leaf_columns = links.gather(leaf_probes, "row")
    leaf_solved = product("lab,lbp->lap", leaf_inverse, leaf_columns).astype(bf16)
    leaf_whole = links.gather(leaf_solved, "row")
    leaf_update = product("lkb,lbp->lkp", leaf_panel, leaf_whole).astype(bf16)
    received = links.gather(links.gather(leaf_update, "leaf"), "row")[0]
    added = [
        jnp.dot(
            pickers[m], received[spans[m][0] : spans[m][1]], preferred_element_type=f32
        ).reshape(counts[m], windows[m], probe_count)
        for m in range(3)
    ]
    lower_input = (lower_probes.astype(f32) - added[0]).astype(bf16)
    middle_base = middle_probes.astype(f32) - added[1]
    root_base = root_probes[None].astype(f32) - added[2]

    def own(block, axis):
        piece = block.shape[1] // lax.axis_size(axis)
        return lax.dynamic_slice_in_dim(block, lax.axis_index(axis) * piece, piece, axis=1)

    lower_columns = links.gather(lower_input, "row")
    lower_block = links.everywhere(product("smn,snp->smp", lower_inverse, lower_columns), "leaf")
    lower_solved = own(lower_block, "leaf").astype(f32)
    to_middle = product("san,snp->sap", lower_to_middle, lower_block)
    to_middle = to_middle.reshape(2, 2, to_middle.shape[1], probe_count).sum(axis=1)
    middle_in = links.everywhere(to_middle, "row", middle_base)
    to_root = product("san,snp->sap", lower_to_root, lower_block).sum(axis=0, keepdims=True)
    middle_block = links.everywhere(product("smn,snp->smp", middle_inverse, middle_in), "leaf")
    middle_solved = own(middle_block, "leaf").astype(f32)
    to_root = to_root + product("san,snp->sap", middle_to_root, middle_block).sum(
        axis=0, keepdims=True
    )
    root_in = links.everywhere(to_root, "row", root_base)
    root_block = links.everywhere(product("smn,snp->smp", root_inverse[None], root_in), "leaf")

    root_columns = links.everywhere(product("smn,smp->snp", root_inverse[None], root_block), "row")
    root_solution = own(root_columns, "row")
    middle_reduced = links.everywhere(
        product("san,ap->snp", middle_to_root, root_columns[0]), "leaf", middle_solved
    )
    middle_columns = links.everywhere(product("smn,smp->snp", middle_inverse, middle_reduced), "row")
    middle_solution = own(middle_columns, "row")
    lower_drop = product("san,ap->snp", lower_to_root, root_columns[0])
    lower_drop = lower_drop + product(
        "san,sap->snp", lower_to_middle, jnp.repeat(middle_columns, 2, axis=0)
    )
    lower_reduced = links.everywhere(lower_drop, "leaf", lower_solved)
    lower_solution = links.total(product("smn,smp->snp", lower_inverse, lower_reduced), "row")

    sources = (lower_solution, middle_solution, root_solution)
    values = jnp.concatenate(
        [
            product("sm,sp->mp", pickers[m], sources[m].reshape(-1, probe_count)).astype(bf16)
            for m in range(3)
        ]
    )
    ancestor = links.total(links.total(values[None], "row"), "leaf")
    leaf_reduced = links.total(
        product("lkb,lkp->lbp", leaf_panel, ancestor), "row", leaf_solved.astype(f32)
    )
    leaf_solution = links.total(product("lab,lap->lbp", leaf_inverse, leaf_reduced), "row")
    return (leaf_solution, lower_solution, middle_solution, root_solution[0])


def solution(mesh):
    placed = (
        P("leaf", "row", None),
        P(None, ("leaf", "row"), None),
        P(None, ("leaf", "row"), None),
        P(("leaf", "row"), None),
        P("leaf", "row", None),
        P(None, "row", "leaf"),
        P(None, "row", "leaf"),
        P("row", "leaf"),
        P("leaf", "row", None),
        P(None, "leaf", "row"),
        P(None, "leaf", "row"),
        P(None, "leaf", "row"),
        P(),
        P(),
    )
    return jax.shard_map(
        body,
        mesh=mesh,
        in_specs=placed,
        out_specs=(
            P("leaf", "row", None),
            P(None, ("leaf", "row"), None),
            P(None, ("leaf", "row"), None),
            P(("leaf", "row"), None),
        ),
        check_vma=False,
    )
```

```python
import functools

import jax
import jax.numpy as jnp
from jax import lax
from jax.experimental import pallas as pl
from jax.experimental.pallas import tpu as pltpu
from jax.sharding import PartitionSpec as P

LOWER_ORDER = 4096
MIDDLE_ORDER = 8192
ROOT_ORDER = 16384
BLOCK = 128
PANEL = 512
LEVELS = 4


def exchange_kernel(axis, n, reduce, gather, has_base, terms, cuts, depth, *refs):
    refs = list(refs)
    if terms:
        weights = [refs.pop(0) for _ in terms]
        columns = [refs.pop(0) for _ in terms]
    else:
        parts_ref = refs.pop(0)
    base_ref = refs.pop(0) if has_base else None
    out_ref = refs.pop(0)
    near_land, staged, far_land, whole, sems = refs[:5]
    if terms:
        parts_ref, weight_sems = refs[5], refs[6]
        tiles = refs[7:]
    far_count = n // 2
    me = lax.axis_index(axis)
    near = lax.rem(me, 2)
    far = me // 2
    partner = far * 2 + (1 - near)

    def far_at(k):
        return lax.rem(far + k, far_count)

    def device(index):
        return {axis: index}

    def remote(src, dst, kind, k, cut, target):
        return pltpu.make_async_remote_copy(
            src_ref=src,
            dst_ref=dst,
            send_sem=sems.at[0, kind, k, cut],
            recv_sem=sems.at[1, kind, k, cut],
            device_id=device(target),
            device_id_type=pl.DeviceIdType.MESH,
        )

    order = sorted(range(1, far_count), key=lambda k: -min(k, far_count - k)) + [0]
    pieces = []
    for k in order:
        pieces += [far_at(k) * 2 + (1 - near), far_at(k) * 2 + near]

    def load(step, number):
        w = parts_ref.shape[2]
        span = pl.ds(pl.multiple_of(pieces[step] * w, w), w)
        ref = weights[number]
        src = ref.at[:, :, span] if terms[number] else ref.at[:, span, :]
        slot = step % depth
        return pltpu.make_async_copy(src, tiles[number].at[slot], weight_sems.at[number, slot])

    def compute(step):
        if not terms:
            return
        sums = [None] * parts_ref.shape[0]
        for number, flipped in enumerate(terms):
            load(step, number).wait()
            tile = tiles[number].at[step % depth]
            count = tile.shape[0]
            for member in range(count):
                group = member * len(sums) // count
                if len(columns[number].shape) == 2:
                    column = columns[number][...]
                else:
                    column = columns[number][member * columns[number].shape[0] // count]
                if flipped:
                    one = jnp.dot(column, tile[member], preferred_element_type=jnp.float32)
                    one = one.T
                else:
                    one = jnp.dot(tile[member], column, preferred_element_type=jnp.float32)
                sums[group] = one if sums[group] is None else sums[group] + one
        for group, value in enumerate(sums):
            parts_ref[group, pieces[step]] = value.astype(parts_ref.dtype)
        if step + depth < len(pieces):
            for number in range(len(terms)):
                load(step + depth, number).start()

    if terms:
        for step in range(min(depth, len(pieces))):
            for number in range(len(terms)):
                load(step, number).start()

    barrier = pltpu.get_barrier_semaphore()
    pl.semaphore_signal(
        barrier, inc=1, device_id=device(partner), device_id_type=pl.DeviceIdType.MESH
    )
    for k in range(1, far_count):
        pl.semaphore_signal(
            barrier,
            inc=1,
            device_id=device(far_at(k) * 2 + near),
            device_id_type=pl.DeviceIdType.MESH,
        )
    pl.semaphore_wait(barrier, far_count)

    sends = []
    if reduce:
        to_partner, to_far = {}, {}

        def finish(k):
            to_partner[k].wait_recv()
            pair = parts_ref[:, far_at(k) * 2 + near].astype(jnp.float32) + near_land[k].astype(
                jnp.float32
            )
            if k == 0:
                return pair
            staged[k] = pair.astype(staged.dtype)
            to_far[k] = remote(staged.at[k], far_land.at[k], 1, k, 0, far_at(k) * 2 + near)
            to_far[k].start()
            return None

        for t, k in enumerate(order):
            compute(2 * t)
            to_partner[k] = remote(
                parts_ref.at[:, far_at(k) * 2 + (1 - near)], near_land.at[k], 0, k, 0, partner
            )
            to_partner[k].start()
            compute(2 * t + 1)
            if t >= 1:
                finish(order[t - 1])
        total = finish(0)
        for k in order[:-1]:
            to_far[k].wait_recv()
            total = total + far_land[k].astype(jnp.float32)
        if has_base:
            total = base_ref[...] - total
        mine = total.astype(out_ref.dtype)
        sends += [to_partner[k] for k in order] + [to_far[k] for k in order[:-1]]
    else:
        mine = parts_ref[...]
    if gather:
        whole[:, me] = mine
        rows = whole.shape[2] // cuts

        def spread(owner, kind, k, cut, target):
            part = whole.at[:, owner, cut * rows : (cut + 1) * rows]
            copy = remote(part, part, kind, k, cut, target)
            copy.start()
            sends.append(copy)
            return copy

        along, passed = {}, []
        for cut in range(cuts):
            for k in order[:-1]:
                along[k, cut] = spread(me, 2, k, cut, far_at(k) * 2 + near)
            passed.append(spread(me, 3, 0, cut, partner))
        for cut in range(cuts):
            for k in reversed(order[:-1]):
                along[k, cut].wait_recv()
                came = lax.rem(far + far_count - k, far_count) * 2 + near
                passed.append(spread(came, 3, k, cut, partner))
        for copy in passed:
            copy.wait_recv()
    for copy in sends:
        copy.wait_send()
    out_ref[...] = whole[...] if gather else mine


class Exchanges:
    def __init__(self):
        self.calls = 0

    def run(self, parts, axis, reduce, gather, base=None, terms=None):
        n = lax.axis_size(axis)
        far_count = n // 2
        flips, extra, depth = (), [], 0
        if terms:
            s, rows, p = parts
            w = rows // n
            flips = tuple(flipped for _, _, flipped in terms)
            operands = [weight for weight, _, _ in terms]
            operands += [
                jnp.swapaxes(x, -1, -2) if flipped else x for _, x, flipped in terms
            ]
            tile_shapes = [
                (q.shape[0], q.shape[1], w) if flipped else (q.shape[0], w, q.shape[2])
                for q, _, flipped in terms
            ]
            depth = 3 if sum(a * b * c for a, b, c in tile_shapes) <= (1 << 20) else 2
            extra = [pltpu.VMEM((s, n, w, p), jnp.bfloat16)]
            extra += [pltpu.SemaphoreType.DMA((len(terms), depth))]
            extra += [pltpu.VMEM((depth,) + t, jnp.bfloat16) for t in tile_shapes]
        elif reduce:
            s, rows, p = parts.shape
            w = rows // n
            operands = [parts.astype(jnp.bfloat16).reshape(s, n, w, p)]
        else:
            s, w, p = parts.shape
            operands = [parts]
        specs = [
            pl.BlockSpec(memory_space=pl.ANY if i < len(flips) else pltpu.VMEM)
            for i in range(len(operands))
        ]
        if base is not None:
            operands.append(base)
            specs.append(pl.BlockSpec(memory_space=pltpu.VMEM))
        slots = (far_count if reduce else 1, s if reduce else 1, w if reduce else 16, p)
        out_shape = (s, n, w, p) if gather else (s, w, p)
        whole_shape = (s, n, w, p) if gather else (1, 1, 16, p)
        cuts = 4 if far_count > 2 and w % 64 == 0 and s * w >= 512 else 1
        call_id = self.calls
        self.calls += 1
        out = pl.pallas_call(
            functools.partial(
                exchange_kernel, axis, n, reduce, gather, base is not None, flips, cuts, depth
            ),
            out_shape=jax.ShapeDtypeStruct(out_shape, jnp.bfloat16),
            in_specs=specs,
            out_specs=pl.BlockSpec(memory_space=pltpu.VMEM),
            scratch_shapes=[
                pltpu.VMEM(slots, jnp.bfloat16),
                pltpu.VMEM(slots, jnp.bfloat16),
                pltpu.VMEM(slots, jnp.bfloat16),
                pltpu.VMEM(whole_shape, jnp.bfloat16),
                pltpu.SemaphoreType.DMA((2, 4, far_count, cuts)),
            ]
            + extra,
            compiler_params=pltpu.CompilerParams(
                collective_id=call_id,
                has_side_effects=True,
                vmem_limit_bytes=(40 << 20) if terms else (16 << 20),
            ),
            name=f"exchange_{axis}_{call_id}",
        )(*operands)
        return out.reshape(s, n * w, p) if gather else out

    def gather(self, pieces, axis):
        return self.run(pieces, axis, False, True)

    def total(self, summands, axis, base=None):
        return self.run(summands, axis, True, False, base)

    def everywhere(self, groups, rows, terms, axis, base=None):
        probe_count = terms[0][1].shape[-1]
        w = rows // lax.axis_size(axis)
        if not any(flipped for _, _, flipped in terms) or w % 128 == 0:
            return self.run((groups, rows, probe_count), axis, True, True, base, terms)
        summands = 0.0
        for weight, x, flipped in terms:
            count = weight.shape[0]
            if x.ndim == 2:
                x = x[None]
            x = jnp.repeat(x, count // x.shape[0], axis=0)
            one = product("smn,smp->snp" if flipped else "smn,snp->smp", weight, x)
            summands += one.reshape(groups, count // groups, rows, probe_count).sum(axis=1)
        return self.run(summands, axis, True, True, base)


def product(spec, left, right):
    return jnp.einsum(spec, left, right, preferred_element_type=jnp.float32)


def target_places(leaf_parent, leaf_blocks, block_index):
    offset = jnp.arange(BLOCK, dtype=jnp.int32)[None, :]
    owners = leaf_parent if block_index < 2 else leaf_parent // 2
    if block_index == 3:
        owners = jnp.zeros_like(leaf_parent)
    owners = owners[:, None] + 0 * offset
    return owners, leaf_blocks[:, block_index : block_index + 1] * BLOCK + offset


def picker(leaf_parent, leaf_blocks, block_indices, row_devices, separators, start, window):
    slots = []
    for block_index in block_indices:
        owners, places = target_places(leaf_parent, leaf_blocks, block_index)
        inside = (places >= start) & (places < start + window)
        slot = jnp.where(inside, owners * window + places - start, -1)
        leaves = slot.shape[0]
        pieces = row_devices // LEVELS
        slots.append(slot.reshape(leaves, pieces, BLOCK // pieces).transpose(1, 0, 2).reshape(-1))
    slot = jnp.concatenate(slots)
    slot_ids = jnp.arange(separators * window, dtype=jnp.int32)
    return (slot_ids[:, None] == slot[None, :]).astype(jnp.bfloat16)


def body(
    leaf_probes,
    lower_probes,
    middle_probes,
    root_probes,
    leaf_inverse,
    lower_inverse,
    middle_inverse,
    root_inverse,
    leaf_panel,
    lower_to_middle,
    lower_to_root,
    middle_to_root,
    leaf_parent,
    leaf_blocks,
):
    f32, bf16 = jnp.float32, jnp.bfloat16
    links = Exchanges()
    leaf_devices = lax.axis_size("leaf")
    row_devices = lax.axis_size("row")
    position = lax.axis_index("leaf") * row_devices + lax.axis_index("row")
    devices = leaf_devices * row_devices
    probe_count = leaf_probes.shape[-1]
    counts = (4, 2, 1)
    windows = [order // devices for order in (LOWER_ORDER, MIDDLE_ORDER, ROOT_ORDER)]
    blocks_of = ((0, 1), (2,), (3,))
    pickers = [
        picker(
            leaf_parent,
            leaf_blocks,
            blocks_of[m],
            row_devices,
            counts[m],
            position * windows[m],
            windows[m],
        )
        for m in range(3)
    ]
    per_block = leaf_devices * BLOCK
    spans = ((0, 2 * per_block), (2 * per_block, 3 * per_block), (3 * per_block, 4 * per_block))

    leaf_columns = links.gather(leaf_probes, "row")
    leaf_solved = product("lab,lbp->lap", leaf_inverse, leaf_columns).astype(bf16)
    leaf_whole = links.gather(leaf_solved, "row")
    leaf_update = product("lkb,lbp->lkp", leaf_panel, leaf_whole).astype(bf16)
    received = links.gather(links.gather(leaf_update, "leaf"), "row")[0]
    added = [
        jnp.dot(
            pickers[m], received[spans[m][0] : spans[m][1]], preferred_element_type=f32
        ).reshape(counts[m], windows[m], probe_count)
        for m in range(3)
    ]
    lower_input = (lower_probes.astype(f32) - added[0]).astype(bf16)
    middle_base = middle_probes.astype(f32) - added[1]
    root_base = root_probes[None].astype(f32) - added[2]

    def own(block, axis):
        piece = block.shape[1] // lax.axis_size(axis)
        return lax.dynamic_slice_in_dim(block, lax.axis_index(axis) * piece, piece, axis=1)

    lower_columns = links.gather(lower_input, "row")
    lower_rows, lower_width = lower_inverse.shape[1:]
    middle_rows, middle_width = middle_inverse.shape[1:]
    root_rows, root_width = root_inverse.shape
    lower_block = links.everywhere(4, lower_rows, [(lower_inverse, lower_columns, False)], "leaf")
    lower_solved = own(lower_block, "leaf").astype(f32)
    middle_in = links.everywhere(
        2, middle_width, [(lower_to_middle, lower_block, False)], "row", middle_base
    )
    middle_block = links.everywhere(2, middle_rows, [(middle_inverse, middle_in, False)], "leaf")
    middle_solved = own(middle_block, "leaf").astype(f32)
    root_in = links.everywhere(
        1,
        root_width,
        [(lower_to_root, lower_block, False), (middle_to_root, middle_block, False)],
        "row",
        root_base,
    )
    root_block = links.everywhere(1, root_rows, [(root_inverse[None], root_in, False)], "leaf")

    root_columns = links.everywhere(1, root_width, [(root_inverse[None], root_block, True)], "row")
    root_solution = own(root_columns, "row")
    middle_reduced = links.everywhere(
        2, middle_rows, [(middle_to_root, root_columns, True)], "leaf", middle_solved
    )
    middle_columns = links.everywhere(
        2, middle_width, [(middle_inverse, middle_reduced, True)], "row"
    )
    middle_solution = own(middle_columns, "row")
    lower_reduced = links.everywhere(
        4,
        lower_rows,
        [(lower_to_root, root_columns, True), (lower_to_middle, middle_columns, True)],
        "leaf",
        lower_solved,
    )
    lower_solution = links.total(product("smn,smp->snp", lower_inverse, lower_reduced), "row")

    sources = (lower_solution, middle_solution, root_solution)
    values = jnp.concatenate(
        [
            product("sm,sp->mp", pickers[m], sources[m].reshape(-1, probe_count)).astype(bf16)
            for m in range(3)
        ]
    )
    ancestor = links.total(links.total(values[None], "row"), "leaf")
    leaf_reduced = links.total(
        product("lkb,lkp->lbp", leaf_panel, ancestor), "row", leaf_solved.astype(f32)
    )
    leaf_solution = links.total(product("lab,lap->lbp", leaf_inverse, leaf_reduced), "row")
    return (leaf_solution, lower_solution, middle_solution, root_solution[0])


def solution(mesh):
    placed = (
        P("leaf", "row", None),
        P(None, ("leaf", "row"), None),
        P(None, ("leaf", "row"), None),
        P(("leaf", "row"), None),
        P("leaf", "row", None),
        P(None, "row", "leaf"),
        P(None, "row", "leaf"),
        P("row", "leaf"),
        P("leaf", "row", None),
        P(None, "leaf", "row"),
        P(None, "leaf", "row"),
        P(None, "leaf", "row"),
        P(),
        P(),
    )
    return jax.shard_map(
        body,
        mesh=mesh,
        in_specs=placed,
        out_specs=(
            P("leaf", "row", None),
            P(None, ("leaf", "row"), None),
            P(None, ("leaf", "row"), None),
            P(("leaf", "row"), None),
        ),
        check_vma=False,
    )
```
